256 devices in a mesh: section: 2 (over x_lo), dp: 8 (over z), tensor: 16 (over x_hi, y, core).
Axes of the slice: x: 4 (x_hi: 2, x_lo: 2; x = x_hi * 2 + x_lo), y: 4, z: 8, core: 2. Of those that a mesh axis runs over, the one named last changes fastest.
Arguments:
- grads: bfloat16 [2, 8192, 8192], P('section', 'dp', 'tensor')
- groups: int32 [2, 8192], P('section', 'tensor'), may hold values from 0 to 3
- acts: bfloat16 [2, 8192, 14336], P('section', 'dp', 'tensor'), may hold values from -6 to 6
Outputs:
- hessian: float32 [2, 14336, 3584], P('section', ('tensor', 'dp'))
The draws below stay inside these ranges and needn't reach their ends.
All inputs are finite; a program needn't handle non-finite values.
Results may differ from the reference program's by a relative error of at most 0.0009.
Values may be sent and summed in bfloat16 or wider, within the bound.
No kernel may reach another device: no remote copies, remote signals or barrier semaphores. Data moves between devices by JAX's collectives and lax.ppermute only.
A program may use at most 256 MiB of HBM per device.

```python
import jax
import jax.numpy as jnp
from jax import lax

D = 8192
HID_DEV = 896
GROUPS = 4
TOKENS = 8192
HIDWIN = 14336
N_SECTION = 2


def draw_grads(key, part):
    key = jax.random.fold_in(key, 11)
    column = jnp.arange(D, dtype=jnp.float32) / D
    spread = (0.5 + 1.5 * column)[None, None, :]
    values = jax.random.normal(key, (N_SECTION, TOKENS, D), jnp.float32) * spread
    return values.astype(jnp.bfloat16)


def place_ends(drawn, stream_key, smallest, high):
    index_at = [jax.random.randint(jax.random.fold_in(stream_key, axis), (), 0, length) for axis, length in enumerate(drawn.shape)]
    widest = drawn.shape.index(max(drawn.shape))
    beside = index_at[:widest] + [(index_at[widest] + 1) % drawn.shape[widest]] + index_at[widest + 1:]
    return drawn.at[tuple(index_at)].set(smallest).at[tuple(beside)].set(high)


def shard_levels(rng, extent, pieces, least, largest):
    level = 1.0
    for position, parts in pieces:
        draws = jax.random.uniform(jax.random.fold_in(jax.random.fold_in(rng, 6), position), (parts,), jnp.float32, least / len(pieces), largest / len(pieces))
        level = level * jnp.repeat(jnp.exp(draws), extent[position] // parts).reshape((-1,) + (1,) * (len(extent) - 1 - position))
    return level


def scatter_about(own_key, dims, scale, bound, split=(), kind=jnp.bfloat16):
    loudness = shard_levels(own_key, dims, split, -0.22, 0.18) if split else 1.0
    drawn = jax.random.normal(own_key, dims, jnp.float32) * scale * loudness
    return jnp.minimum(jnp.maximum(drawn, -bound), bound).astype(kind)


def setup_inputs(seed: int = 0) -> dict:
    splits = jax.random.split(jax.random.key(seed), 4)
    return {
        "grads": draw_grads(jax.random.fold_in(splits[3], 71), 0),
        "groups": place_ends(jax.random.randint(splits[1], (N_SECTION, D), 0, GROUPS), jax.random.fold_in(splits[1], 1), 0, GROUPS - 1).astype(jnp.int32),
        "acts": scatter_about(splits[2], (N_SECTION, TOKENS, HIDWIN), 1.0, 6.0, ((0, 2), (1, 8), (2, 16))),
    }


def section_hessian(grad_sum, group_row, act_rows):
    onehot = (group_row[:, None] == jnp.arange(GROUPS, dtype=jnp.int32)[None, :]).astype(jnp.float32)
    squares = grad_sum * grad_sum
    weight = jnp.dot(squares, onehot, precision=lax.Precision.HIGHEST) / D

    def one_block(block):
        cols = lax.dynamic_slice_in_dim(act_rows, block * HID_DEV, HID_DEV, 1)
        scaled = (weight[:, :, None] * cols[:, None, :]).astype(jnp.bfloat16)
        scaled = scaled.reshape(cols.shape[0], GROUPS * HID_DEV)
        summed = lax.dot_general(cols, scaled, (((0,), (0,)), ((), ())), preferred_element_type=jnp.float32)
        return summed * (1.0 / TOKENS)

    blocks = lax.map(one_block, jnp.arange(HIDWIN // HID_DEV, dtype=jnp.int32))
    return blocks.reshape(HIDWIN, GROUPS * HID_DEV)


def reference(grads, groups, acts):
    wide = grads.astype(jnp.float32)
    outgrad = jnp.cumsum(wide[::-1], axis=0)[::-1]
    results = []
    for layer in range(grads.shape[0]):
        results.append(section_hessian(outgrad[layer], groups[layer], acts[layer]))
    return jnp.stack(results, 0)
```

```python
import jax
import jax.numpy as jnp
from jax import lax
from jax.experimental import pallas as pl
from jax.experimental.pallas import tpu as pltpu
from jax.sharding import PartitionSpec as P

D = 8192
GROUPS = 4
MICRO = 4
DP = 8
SENT = jnp.float16
VMEM_LIMIT = 48 * 1024 * 1024


def shift(value, axis, steps):
    count = lax.axis_size(axis)
    return lax.ppermute(value, axis, [(i, (i + steps) % count) for i in range(count)])


def square_kernel(groups_ref, own_ref, other_ref, out_ref):
    group = lax.broadcasted_iota(jnp.int32, (16, groups_ref.shape[1]), 0)
    onehot = jnp.where(groups_ref[...] == group, 1.0, 0.0).astype(jnp.bfloat16)
    total = own_ref[...].astype(jnp.float32) + other_ref[...].astype(jnp.float32)
    rest = total * total
    result = jnp.zeros((16, own_ref.shape[0]), jnp.float32)
    for _ in range(3):
        part = rest.astype(jnp.bfloat16)
        rest = rest - part.astype(jnp.float32)
        result += lax.dot_general(
            onehot, part, (((1,), (1,)), ((), ())), preferred_element_type=jnp.float32
        )
    out_ref[...] = result[:8]


def group_squares(groups, own, other):
    return pl.pallas_call(
        square_kernel,
        out_shape=jax.ShapeDtypeStruct((8, own.shape[0]), jnp.float32),
        compiler_params=pltpu.CompilerParams(vmem_limit_bytes=VMEM_LIMIT),
    )(groups, own, other)


def scale_kernel(weight_ref, acts_ref, rows_ref, scaled_ref, product_ref):
    width = acts_ref.shape[1]
    acts = acts_ref[...].astype(jnp.float32)

    @pl.when(pl.program_id(0) == 0)
    def _():
        product_ref[...] = jnp.zeros_like(product_ref)

    for g in range(GROUPS):
        cols = slice(g * width, (g + 1) * width)
        scaled = (weight_ref[:, g : g + 1] * acts).astype(jnp.bfloat16)
        scaled_ref[:, cols] = scaled
        product_ref[:, cols] += jnp.dot(rows_ref[...], scaled, preferred_element_type=jnp.float32)


def scale_and_first(weight, acts, rows):
    tokens, width = acts.shape
    block = 256
    return pl.pallas_call(
        scale_kernel,
        grid=(tokens // block,),
        in_specs=[
            pl.BlockSpec((block, GROUPS), lambda k: (k, 0)),
            pl.BlockSpec((block, width), lambda k: (k, 0)),
            pl.BlockSpec((rows.shape[0], block), lambda k: (0, k)),
        ],
        out_specs=[
            pl.BlockSpec((block, GROUPS * width), lambda k: (k, 0)),
            pl.BlockSpec((rows.shape[0], GROUPS * width), lambda k: (0, 0)),
        ],
        out_shape=[
            jax.ShapeDtypeStruct((tokens, GROUPS * width), jnp.bfloat16),
            jax.ShapeDtypeStruct((rows.shape[0], GROUPS * width), jnp.float32),
        ],
        compiler_params=pltpu.CompilerParams(vmem_limit_bytes=VMEM_LIMIT),
    )(weight, acts, rows)


def product_kernel(rows_ref, scaled_ref, out_ref):
    out_ref[...] = jnp.dot(rows_ref[...], scaled_ref[...], preferred_element_type=jnp.float32)


def product(rows, scaled):
    tokens, cols = scaled.shape
    count = rows.shape[0]
    block = cols // GROUPS
    return pl.pallas_call(
        product_kernel,
        grid=(GROUPS,),
        in_specs=[
            pl.BlockSpec((count, tokens), lambda g: (0, 0)),
            pl.BlockSpec((tokens, block), lambda g: (0, g)),
        ],
        out_specs=pl.BlockSpec((count, block), lambda g: (0, g)),
        out_shape=jax.ShapeDtypeStruct((count, cols), jnp.float32),
        compiler_params=pltpu.CompilerParams(vmem_limit_bytes=VMEM_LIMIT),
        cost_estimate=pl.CostEstimate(
            flops=2 * count * tokens * cols,
            bytes_accessed=2 * tokens * cols + 4 * count * cols,
            transcendentals=0,
        ),
    )(rows, scaled)


def on_device(grads, groups, acts):
    me = lax.axis_index("dp")
    own = grads[0]
    tokens = own.shape[0]
    step = tokens // MICRO

    partial = []
    for index in range(MICRO):
        piece = own[index * step : (index + 1) * step]
        later = lax.ppermute(piece, "section", [(1, 0)])
        partial.append(group_squares(groups, piece, later)[:GROUPS])
    partial = jnp.concatenate(partial, 1)
    count = lax.axis_size("tensor")
    spread = jnp.broadcast_to(partial[None], (count, GROUPS, tokens))
    weight = lax.all_to_all(spread, "tensor", 0, 0, tiled=True).sum(0) / D

    cols = acts[0]
    width = cols.shape[1]
    rows = width // DP
    turned = cols.T
    peak = jnp.max(jnp.abs(turned), axis=0).astype(jnp.float32)
    blocks = [
        lax.dynamic_slice_in_dim(turned, ((me + k) % DP) * rows, rows, 0) for k in range(DP)
    ]

    top = jnp.maximum(jnp.max(weight * (peak * peak)[None]), 1e-30)
    top = jnp.broadcast_to(top, (8, 128))
    top_left, top_right = shift(top, "dp", 1), shift(top, "dp", -1)
    near = jnp.maximum(top, jnp.maximum(top_left, top_right))
    every = jnp.maximum(near, jnp.maximum(shift(near, "dp", 3), shift(near, "dp", -3)))
    own_scale = (32768.0 / tokens) / top[0, 0]
    left_back = (tokens / 32768.0) * top_left[0, 0]
    right_back = (tokens / 32768.0) * top_right[0, 0]
    all_scale = (32768.0 / (tokens * DP)) / every[0, 0]
    all_back = (tokens * DP / 32768.0) * every[0, 0]

    scaled, far = scale_and_first(weight.T, cols, blocks[4])
    third = product(jnp.concatenate([blocks[3], blocks[5]], 0), scaled)
    second = product(jnp.concatenate([blocks[2], blocks[6]], 0), scaled)
    first = product(jnp.concatenate([blocks[1], blocks[7]], 0), scaled)
    mine = product(blocks[0], scaled)

    half = GROUPS * width // 2
    a, b = slice(0, half), slice(half, 2 * half)
    up, down = slice(0, rows), slice(rows, 2 * rows)

    def pack(value, scale):
        return (value * scale).astype(SENT)

    def unpack(value, back):
        return value.astype(jnp.float32) * back

    def send(value, steps):
        return shift(value, "dp", steps)

    r1 = send(pack(far[:, a], own_scale), 1)
    l1 = send(pack(far[:, b], own_scale), -1)
    r2 = send(pack(third[up, b], own_scale), 1)
    l2 = send(pack(third[down, a], own_scale), -1)
    r3 = send(pack(third[up, a] + unpack(r1, left_back), all_scale), 1)
    l3 = send(pack(third[down, b] + unpack(l1, right_back), all_scale), -1)
    r4 = send(pack(second[up, b] + unpack(r2, left_back), all_scale), 1)
    l4 = send(pack(second[down, a] + unpack(l2, right_back), all_scale), -1)
    r5 = send(pack(second[up, a] + unpack(r3, all_back), all_scale), 1)
    l5 = send(pack(second[down, b] + unpack(l3, all_back), all_scale), -1)
    r6 = send(pack(first[up, b] + unpack(r4, all_back), all_scale), 1)
    l6 = send(pack(first[down, a] + unpack(l4, all_back), all_scale), -1)
    r7 = send(pack(first[up, a] + unpack(r5, all_back), all_scale), 1)
    l7 = send(pack(first[down, b] + unpack(l5, all_back), all_scale), -1)

    factor = 1.0 / (tokens * DP)
    left = mine[:, a] + (unpack(r7, all_back) + unpack(l6, all_back))
    right = mine[:, b] + (unpack(r6, all_back) + unpack(l7, all_back))
    return (jnp.concatenate([left, right], 1) * factor)[None]


def solution(mesh):
    return jax.shard_map(
        on_device,
        mesh=mesh,
        in_specs=(
            P("section", "dp", "tensor"),
            P("section", "tensor"),
            P("section", "dp", "tensor"),
        ),
        out_specs=P("section", ("tensor", "dp"), None),
        check_vma=False,
    )
```

```python
import functools

import jax
import jax.numpy as jnp
from jax import lax
from jax.experimental import pallas as pl
from jax.experimental.pallas import tpu as pltpu
from jax.sharding import PartitionSpec as P

D = 8192
GROUPS = 4
DP = 8
LANES = 128
SENT = jnp.float16
VMEM_LIMIT = 48 * 1024 * 1024
KEPT = (384, 256)


def shift(value, axis, steps):
    count = lax.axis_size(axis)
    return lax.ppermute(value, axis, [(i, (i + steps) % count) for i in range(count)])


def square_kernel(groups_ref, own_ref, *refs):
    group = lax.broadcasted_iota(jnp.int32, (16, groups_ref.shape[1]), 0)
    onehot = jnp.where(groups_ref[...] == group, 1.0, 0.0).astype(jnp.bfloat16)
    total = own_ref[...].astype(jnp.float32)
    if len(refs) == 2:
        total = total + refs[0][...].astype(jnp.float32)
    rest = total * total
    result = jnp.zeros((16, own_ref.shape[0]), jnp.float32)
    for _ in range(3):
        part = rest.astype(jnp.bfloat16)
        rest = rest - part.astype(jnp.float32)
        result += lax.dot_general(
            onehot, part, (((1,), (1,)), ((), ())), preferred_element_type=jnp.float32
        )
    refs[-1][...] = result[:GROUPS]


def group_squares(groups, *parts):
    return pl.pallas_call(
        square_kernel,
        out_shape=jax.ShapeDtypeStruct((GROUPS, parts[0].shape[0]), jnp.float32),
        compiler_params=pltpu.CompilerParams(vmem_limit_bytes=VMEM_LIMIT),
    )(groups, *parts)


def section_weights(own, groups):
    tokens = own.shape[0]
    keep = sum(KEPT)
    pieces, start = [], 0
    for size in KEPT:
        pieces.append(own[start : start + size])
        start += size
    moved = own[keep:]
    first_groups = lax.ppermute(groups, "section", [(0, 1)])
    first = lax.ppermute(moved, "section", [(0, 1)])
    later = [lax.ppermute(piece, "section", [(1, 0)]) for piece in pieces]
    alone = group_squares(groups, moved)
    back = lax.ppermute(group_squares(first_groups, moved, first), "section", [(1, 0)])
    partial = [group_squares(groups, piece, other) for piece, other in zip(pieces, later)]
    partial.append(jnp.where(lax.axis_index("section") == 0, back, alone))
    partial = jnp.concatenate(partial, 1)
    count = lax.axis_size("tensor")
    partial += lax.ppermute(partial, "tensor", [(i, i ^ 1) for i in range(count)])
    chips = [list(range(core, count, 2)) for core in (0, 1)]
    spread = jnp.broadcast_to(partial[None], (count // 2, GROUPS, tokens))
    spread = lax.all_to_all(spread, "tensor", 0, 0, axis_index_groups=chips, tiled=True)
    return spread.sum(0) / D


def product_kernel(order, me_ref, weight_ref, turned_ref, *refs):
    rows_ref = refs[-1]
    outs = refs[:-1]
    group = pl.program_id(0)
    me = me_ref[0]
    count = outs[-1].shape[2]
    low = group < GROUPS // 2

    @pl.when(group % (GROUPS // 2) == 0)
    def _():
        for n, (first, second, _) in enumerate(order):
            at = lax.rem(me + jnp.where(low, first, second), DP) * count
            rows_ref[n * count : (n + 1) * count, :] = turned_ref[
                pl.ds(pl.multiple_of(at, 16), count), :
            ]

    weight = weight_ref[pl.ds(group, 1), :]
    scaled = (turned_ref[...].astype(jnp.float32) * weight).astype(jnp.bfloat16)
    result = lax.dot_general(
        rows_ref[...], scaled, (((1,), (1,)), ((), ())), preferred_element_type=jnp.float32
    )
    for n in range(len(order)):
        for c in range(outs[n].shape[1]):
            outs[n][0, c] = result[n * count : (n + 1) * count, c * LANES : (c + 1) * LANES]


def products(me, weight, turned, *order):
    width, tokens = turned.shape
    count = width // DP
    tiles = width // LANES
    half = GROUPS // 2 * tiles
    block = (1, tiles, count, LANES)
    split = pl.BlockSpec(block, lambda g, me: (g // 2, g % 2, 0, 0))
    swapped = pl.BlockSpec(block, lambda g, me: (1 - g // 2, g % 2, 0, 0))
    return pl.pallas_call(
        functools.partial(product_kernel, order),
        grid_spec=pltpu.PrefetchScalarGridSpec(
            num_scalar_prefetch=1,
            grid=(GROUPS,),
            in_specs=[
                pl.BlockSpec((GROUPS, tokens), lambda g, me: (0, 0)),
                pl.BlockSpec((width, tokens), lambda g, me: (0, 0)),
            ],
            out_specs=[swapped if first > second else split for first, second, _ in order],
            scratch_shapes=[pltpu.VMEM((len(order) * count, tokens), jnp.bfloat16)],
        ),
        out_shape=[
            jax.ShapeDtypeStruct((2, half + room, count, LANES), jnp.float32)
            for _, _, room in order
        ],
        compiler_params=pltpu.CompilerParams(vmem_limit_bytes=VMEM_LIMIT),
        cost_estimate=pl.CostEstimate(flops=1, bytes_accessed=1, transcendentals=0),
    )(me, weight, turned)


def add_kernel(left_ref, right_ref, out_ref):
    out_ref[...] = left_ref[...] + right_ref[...]


def add(left, right):
    block = pl.BlockSpec((1, *left.shape[1:]), lambda i: (i, 0, 0, 0))
    return pl.pallas_call(
        add_kernel,
        grid=(left.shape[0],),
        in_specs=[block, block],
        out_specs=block,
        out_shape=jax.ShapeDtypeStruct(left.shape, left.dtype),
        compiler_params=pltpu.CompilerParams(vmem_limit_bytes=VMEM_LIMIT),
        cost_estimate=pl.CostEstimate(flops=8_000_000_000, bytes_accessed=1, transcendentals=0),
    )(left, right)


def on_device(grads, groups, acts):
    me = lax.axis_index("dp").astype(jnp.int32).reshape(1)
    weight = section_weights(grads[0], groups)

    cols = acts[0]
    tokens, width = cols.shape
    rows = width // DP
    half = GROUPS // 2 * width // LANES
    turned = cols.T
    peak = jnp.max(jnp.abs(turned), axis=0).astype(jnp.float32)

    top = jnp.max(weight * (peak * peak)[None])
    top = jnp.ceil(jnp.log2(jnp.maximum(top, 1e-30)))
    top = lax.optimization_barrier(jnp.broadcast_to(top, (1, LANES)))
    far, early3 = products(me, weight, turned, (4, 4, 1), (5, 3, 0))

    bits = {k: 15 - (tokens * k - 1).bit_length() for k in (1, 2, 3, 4)}
    room = lax.broadcasted_iota(jnp.int32, (half + 1, rows, LANES), 0) == half

    def pack(value, level, count):
        value = value * jnp.exp2(bits[count] - level)[None]
        if value.shape[0] > half:
            value = jnp.where(room, level[None], value)
        return value.astype(SENT)

    def unpack(value, level, count):
        return value.astype(jnp.float32) * jnp.exp2(level - bits[count])[None]

    def tag_of(value):
        return value[half].astype(jnp.float32)

    way = (1, -1)
    both = (0, 1)

    def send(packed):
        return [shift(packed[i], "dp", way[i]) for i in both]

    odd = send([pack(far[i], top, 1) for i in both])
    packed = [pack(early3[i], top, 1) for i in both]
    even = send(packed)
    weight = lax.optimization_barrier((weight, *packed))[0]
    mine, late3, early2, late2, early1, late1 = rest = products(
        me, weight, turned, (0, 0, 0), (3, 5, 1), (6, 2, 0), (2, 6, 1), (7, 1, 0), (1, 7, 1)
    )
    odd = lax.optimization_barrier((*odd, *rest))[:2]
    for count, early, late in ((2, early2, late3), (3, early1, late2), (4, None, late1)):
        level = [tag_of(odd[i]) for i in both]
        after = [jnp.maximum(top, level[i]) for i in both]
        packed = [
            pack(late[i] + unpack(odd[i], level[i], count - 1), after[i], count) for i in both
        ]
        odd = send(packed)
        if early is not None:
            packed = [
                pack(early[i] + unpack(even[i], level[i], count - 1), after[i], count)
                for i in both
            ]
            even = send(packed)
            odd = lax.optimization_barrier((*odd, *packed))[:2]
    last = [tag_of(odd[i]) for i in both]

    factor = 1.0 / (tokens * DP)
    even = [unpack(even[i], level[i], 3) for i in both]
    odd = [unpack(odd[i][:half], last[i], 4) for i in both]
    total = add(mine, jnp.stack(even[::-1])) + jnp.stack(odd)
    total = jnp.transpose(total, (2, 0, 1, 3)) * factor
    return total.reshape(1, rows, GROUPS * width)


def solution(mesh):
    return jax.shard_map(
        on_device,
        mesh=mesh,
        in_specs=(
            P("section", "dp", "tensor"),
            P("section", "tensor"),
            P("section", "dp", "tensor"),
        ),
        out_specs=P("section", ("tensor", "dp"), None),
        check_vma=False,
    )
```

```python
import functools

import jax
import jax.numpy as jnp
from jax import lax
from jax.experimental import pallas as pl
from jax.experimental.pallas import tpu as pltpu
from jax.sharding import PartitionSpec as P

D = 8192
GROUPS = 4
DP = 8
LANES = 128
OWN = (0, 3, 4, 5)
SENT = jnp.float16
VMEM_LIMIT = 8 * 1024 * 1024
PRODUCT_VMEM_LIMIT = 24 * 1024 * 1024
KEPT = 576


def shift(value, axis, steps):
    count = lax.axis_size(axis)
    return lax.ppermute(value, axis, [(i, (i + steps) % count) for i in range(count)])


def split_kernel(groups_ref, own_ref, kept_ref, moved_ref):
    kept_ref[...] = own_ref[:KEPT]
    moved_ref[: own_ref.shape[0] - KEPT] = own_ref[KEPT:]
    names = groups_ref[...].astype(jnp.float32)
    moved_ref[own_ref.shape[0] - KEPT :] = jnp.broadcast_to(names, (16, names.shape[1])).astype(
        moved_ref.dtype
    )


def split(groups, own):
    tokens, channels = own.shape
    return pl.pallas_call(
        split_kernel,
        out_shape=[
            jax.ShapeDtypeStruct((KEPT, channels), own.dtype),
            jax.ShapeDtypeStruct((tokens - KEPT + 16, channels), own.dtype),
        ],
        compiler_params=pltpu.CompilerParams(vmem_limit_bytes=VMEM_LIMIT),
    )(groups, own)


def square_kernel(start, named, groups_ref, own_ref, *refs):
    count = refs[-1].shape[1]
    total = own_ref[start : start + count].astype(jnp.float32)
    groups = groups_ref[...]
    if len(refs) == 2:
        total = total + refs[0][:count].astype(jnp.float32)
        if named:
            groups = refs[0][count:].astype(jnp.float32).astype(jnp.int32)
    group = lax.broadcasted_iota(jnp.int32, (16, groups_ref.shape[1]), 0)
    onehot = jnp.where(groups == group, 1.0, 0.0).astype(jnp.bfloat16)
    rest = total * total
    result = jnp.zeros((16, count), jnp.float32)
    for _ in range(3):
        part = rest.astype(jnp.bfloat16)
        rest = rest - part.astype(jnp.float32)
        result += lax.dot_general(
            onehot, part, (((1,), (1,)), ((), ())), preferred_element_type=jnp.float32
        )
    refs[-1][...] = result[:GROUPS]


def group_squares(groups, own, start, stop, *other, named=False):
    return pl.pallas_call(
        functools.partial(square_kernel, start, named),
        out_shape=jax.ShapeDtypeStruct((GROUPS, stop - start), jnp.float32),
        compiler_params=pltpu.CompilerParams(vmem_limit_bytes=VMEM_LIMIT),
    )(groups, own, *other)


def section_weights(own, groups, meanwhile):
    tokens = own.shape[0]
    kept, moved = split(groups, own)
    first = lax.ppermute(moved, "section", [(0, 1)])
    later = lax.ppermute(kept, "section", [(1, 0)])
    alone = group_squares(groups, own, KEPT, tokens)
    first, alone, *meanwhile = lax.optimization_barrier((first, alone, *meanwhile))
    back = group_squares(groups, own, KEPT, tokens, first, named=True)
    back = lax.ppermute(back, "section", [(1, 0)])
    rest = jnp.where(lax.axis_index("section") == 0, back, alone)
    partial = jnp.concatenate([group_squares(groups, own, 0, KEPT, later), rest], 1)
    count = lax.axis_size("tensor")
    partial += lax.ppermute(partial, "tensor", [(i, i ^ 1) for i in range(count)])
    chips = [list(range(core, count, 2)) for core in (0, 1)]
    spread = jnp.broadcast_to(partial[None], (count // 2, GROUPS, tokens))
    spread = lax.all_to_all(spread, "tensor", 0, 0, axis_index_groups=chips, tiled=True)
    return spread.sum(0) / D, *meanwhile


def product_kernel(jobs, mode, *refs):
    if mode == "given":
        scaled_ref, turned_ref, *outs = refs
    else:
        weight_ref, turned_ref, *outs = refs
    if mode == "alone":
        peak_ref, top_ref, *outs, scaled_ref = outs
        most = weight_ref[...] * (peak_ref[...] * peak_ref[...])
        most = jnp.max(jnp.max(most, axis=0, keepdims=True), axis=1, keepdims=True)
        most = jnp.ceil(jnp.log2(jnp.maximum(most, 1e-30)))
        top_ref[...] = jnp.broadcast_to(most, top_ref.shape)
    if mode == "whole":
        scaled_ref, *outs = outs
    count = turned_ref.shape[0] // DP
    tiles = DP * count // LANES
    size = tiles * count

    def place(b):
        return slice(b % DP * count, (b % DP + 1) * count)

    def dot(left, right):
        return lax.dot_general(
            left, right, (((1,), (1,)), ((), ())), preferred_element_type=jnp.float32
        )

    needed = set(range(DP)) if mode == "whole" else set()
    if mode == "alone":
        for _, _, _, _, (block, distance) in jobs:
            needed |= {block % DP, (block + distance) % DP}
    means = {}
    for p in (0, 1):
        for b in sorted(needed):
            rows = turned_ref[place(b)].astype(jnp.float32)
            for q in (0, 1):
                g = 2 * p + q
                scaled_ref[g, place(b)] = (rows * weight_ref[g : g + 1]).astype(jnp.bfloat16)
        for n, (out, at, block, half, pair) in enumerate(jobs):
            if half == p:
                right = [scaled_ref[2 * p + q, place(block + c)] for q in (0, 1) for c in OWN]
                result = dot(turned_ref[place(block)], jnp.concatenate(right, 0))
                for c in range(tiles):
                    outs[out][at + c * count : at + (c + 1) * count] = result[
                        :, c * LANES : (c + 1) * LANES
                    ]
            if pair is not None:
                one, two = place(pair[0]), place(pair[0] + pair[1])
                right = jnp.concatenate([scaled_ref[2 * p + q, two] for q in (0, 1)], 0)
                left = jnp.concatenate([scaled_ref[2 * p + q, one] for q in (0, 1)], 0)
                first = dot(turned_ref[one], right)
                second = dot(left, turned_ref[two])
                second = jnp.concatenate([second[:count], second[count:]], 1)
                mean = 0.5 * (first + second)
                if p == 0:
                    means[n] = mean
                    continue
                mean = jnp.concatenate([means[n], mean], 1)
                start = at + (size if half is not None else 0)
                whole = GROUPS * count // LANES
                for c in range(whole):
                    outs[out][start + c * count : start + (c + 1) * count] = mean[
                        :, c * LANES : (c + 1) * LANES
                    ]
                rest = mean[:, whole * LANES :]
                start += whole * count
                outs[out][start : start + count // 2] = jnp.concatenate(
                    [rest[: count // 2], rest[count // 2 :]], 1
                )


def products(mode, factors, turned, shapes, jobs, *peak):
    out_shape = [jax.ShapeDtypeStruct((rows, LANES), jnp.float32) for rows in shapes]
    scaled = (GROUPS, *turned.shape)
    scratch = []
    if mode == "alone":
        out_shape.insert(0, jax.ShapeDtypeStruct((8, LANES), jnp.float32))
        scratch.append(pltpu.VMEM(scaled, jnp.bfloat16))
    if mode == "whole":
        out_shape.insert(0, jax.ShapeDtypeStruct(scaled, jnp.bfloat16))
    return pl.pallas_call(
        functools.partial(product_kernel, jobs, mode),
        out_shape=out_shape,
        scratch_shapes=scratch,
        compiler_params=pltpu.CompilerParams(vmem_limit_bytes=PRODUCT_VMEM_LIMIT),
        cost_estimate=pl.CostEstimate(flops=1, bytes_accessed=1, transcendentals=0),
    )(factors, turned, *peak)


def add_kernel(left_ref, right_ref, out_ref):
    out_ref[...] = left_ref[...] + right_ref[...]


def add(left, right):
    return pl.pallas_call(
        add_kernel,
        out_shape=jax.ShapeDtypeStruct(left.shape, left.dtype),
        compiler_params=pltpu.CompilerParams(vmem_limit_bytes=VMEM_LIMIT),
        cost_estimate=pl.CostEstimate(flops=8_000_000_000, bytes_accessed=1, transcendentals=0),
    )(left, right)


def finish_kernel(factor, me_ref, left_ref, right_ref, *refs):
    *pair_refs, out_ref = refs
    count = out_ref.shape[0]
    size = left_ref.shape[0] // 2
    width = DP * count
    whole = GROUPS * count // LANES
    pairs = []
    for ref in pair_refs:
        parts = [ref[c * count : (c + 1) * count] for c in range(whole)]
        rest = ref[whole * count : whole * count + count // 2]
        rest = jnp.concatenate([rest[:, : LANES // 2], rest[:, LANES // 2 :]], 0)
        pairs.append(jnp.concatenate([*parts, rest], 1))
    for p in (0, 1):
        parts = []
        for at in range(p * size, (p + 1) * size, count):
            parts.append(left_ref[at : at + count] + right_ref[at : at + count])
        own = jnp.concatenate(parts, 1)
        for q in (0, 1):
            g = 2 * p + q
            blocks = [None] * DP
            for n, c in enumerate(OWN):
                at = (q * len(OWN) + n) * count
                blocks[c] = own[:, at : at + count]
            pieces = [pair[:, g * count : (g + 1) * count] for pair in pairs]
            blocks[1], blocks[2] = pieces[0], pieces[1]
            blocks[7], blocks[6] = pieces[2].T, pieces[3].T
            row = jnp.concatenate(blocks, 1)
            row = pltpu.roll(row, me_ref[0] * count, 1)
            out_ref[:, g * width : (g + 1) * width] = row * factor


def finish(me, left, right, pairs, count, factor):
    vmem = pl.BlockSpec(memory_space=pltpu.VMEM)
    return pl.pallas_call(
        functools.partial(finish_kernel, factor),
        in_specs=[pl.BlockSpec(memory_space=pltpu.SMEM)] + [vmem] * (2 + len(pairs)),
        out_specs=vmem,
        out_shape=jax.ShapeDtypeStruct((count, GROUPS * DP * count), jnp.float32),
        compiler_params=pltpu.CompilerParams(vmem_limit_bytes=PRODUCT_VMEM_LIMIT),
    )(me, left, right, *pairs)


def on_device(grads, groups, acts):
    me = lax.axis_index("dp").astype(jnp.int32)
    cols = acts[0]
    tokens, width = cols.shape
    rows = width // DP
    turned = cols.T
    peak = jnp.max(jnp.abs(turned), axis=0, keepdims=True).astype(jnp.float32)
    turned = lax.dynamic_slice_in_dim(jnp.concatenate([turned, turned], 0), me * rows, width, 0)
    weight, turned, peak = section_weights(grads[0], groups, (turned, peak))

    size = width // LANES * rows
    pair = GROUPS * rows * rows // LANES
    long, short = size + pair + 8, pair + 8

    first = [(0, 0, None, None, (3, 2))]
    top, ahead0 = products("alone", weight, turned, [short], first, peak)
    top = top[:1]
    way, both = (1, -1), (0, 1)
    sums = {}
    scaled, sums[1, 0], sums[1, 1], sums[2, 0], sums[2, 1] = products(
        "whole",
        weight,
        turned,
        [long] * 4,
        [
            (0, 0, 4, 0, (2, 2)),
            (1, 0, 4, 1, (4, 2)),
            (2, 0, 3, 1, (3, 1)),
            (3, 0, 5, 0, (4, 1)),
        ],
    )
    bits = 15 - (tokens * DP - 1).bit_length()

    def pack(value, level):
        room = lax.broadcasted_iota(jnp.int32, value.shape, 0) >= value.shape[0] - 8
        return jnp.where(room, level, value * jnp.exp2(bits - level)).astype(SENT)

    def tag_of(value):
        return value[-1:].astype(jnp.float32)

    def unpack(value):
        return value.astype(jnp.float32) * jnp.exp2(tag_of(value) - bits)

    def send(packed):
        return [shift(packed[i], "dp", way[i]) for i in both]

    start = shift(pack(ahead0, top), "dp", 1)
    got, sent = {}, {}
    begun = jnp.pad(unpack(start)[:pair], ((size, 8), (0, 0)))
    sent[2] = [pack(sums[2, i], top) for i in both]
    got[2] = send(sent[2])
    sent[1] = [pack(sums[1, 0] + begun, jnp.maximum(top, tag_of(start))), pack(sums[1, 1], top)]
    got[1] = send(sent[1])

    def later(*steps):
        nonlocal scaled
        scaled = lax.optimization_barrier((scaled, *(v for pair in sent.values() for v in pair)))[0]
        jobs, shapes = [], []
        for k in steps:
            for i in both:
                n = len(shapes)
                if k == 0:
                    jobs.append((len(steps) * 2 - 2, i * size, 0, i, None))
                    continue
                if k % 2:
                    pair_of = ((4 - k // 2 - 2, k // 2 - 4)[i], 2)
                else:
                    pair_of = ((4 - k // 2, k // 2 - 5)[i], 1)
                if k == 8:
                    jobs.append((n, 0, None, None, pair_of))
                    shapes.append(short)
                else:
                    block = {3: 3, 4: 2, 5: 2, 6: 1, 7: 1}[k] * way[i]
                    jobs.append((n, 0, block, (k + 1 + i) % 2, pair_of))
                    shapes.append(long)
        if 0 in steps:
            shapes.append(2 * size)
        result = products("given", scaled, turned, shapes, jobs)
        for n, k in enumerate(steps):
            for i in both if k else ():
                sums[k, i] = result[2 * n + i]
        return result

    def tie(k, *others):
        got[k] = lax.optimization_barrier((*got[k], *others))[:2]

    tie(1, *later(3, 4))
    kept = {}
    for k in (3, 4, 5, 6, 7, 8):
        value, sent[k] = [], []
        for i in both:
            before = unpack(got[k - 2][i])
            if k == 8:
                before = before[size:]
            value.append(sums[k, i] + before)
            sent[k].append(pack(value[i], jnp.maximum(top, tag_of(got[k - 2][i]))))
        got[k] = send(sent[k])
        if k == 5:
            kept[k] = [v[size : size + pair] for v in value]
        elif k == 8:
            kept[k] = [v[:pair] for v in value]
        if k == 3:
            tie(2, *later(5, 6))
        elif k == 4:
            *_, mine = last = later(7, 8, 0)
            tie(3, *last)
        if k in (5, 6, 7):
            tie(4 if k == 5 else 5 if k == 6 else 6, *sent[k])

    factor = 1.0 / (tokens * DP)
    even = jnp.concatenate([unpack(got[6][i])[:size] for i in (1, 0)], 0)
    odd = [unpack(got[7][i]) for i in both]
    last = [unpack(got[8][i])[:pair] for i in both]
    pairs = [
        kept[8][0] + last[1],
        kept[5][0] + odd[1][size : size + pair],
        kept[8][1] + last[0],
        kept[5][1] + odd[0][size : size + pair],
    ]
    odd = jnp.concatenate([value[:size] for value in odd], 0)
    return finish(me.reshape(1), add(mine, even), odd, pairs, rows, factor)[None]


def solution(mesh):
    return jax.shard_map(
        on_device,
        mesh=mesh,
        in_specs=(
            P("section", "dp", "tensor"),
            P("section", "tensor"),
            P("section", "dp", "tensor"),
        ),
        out_specs=P("section", ("tensor", "dp"), None),
        check_vma=False,
    )
```

```python
import functools

import jax
import jax.numpy as jnp
from jax import lax
from jax.experimental import pallas as pl
from jax.experimental.pallas import tpu as pltpu
from jax.sharding import PartitionSpec as P

D = 8192
GROUPS = 4
DP = 8
LANES = 128
OWN = (0, 3, 4, 5)
SENT = jnp.float16
VMEM_LIMIT = 8 * 1024 * 1024
PRODUCT_VMEM_LIMIT = 24 * 1024 * 1024
KEPT = 576


def shift(value, axis, steps):
    count = lax.axis_size(axis)
    return lax.ppermute(value, axis, [(i, (i + steps) % count) for i in range(count)])


def split_kernel(groups_ref, own_ref, kept_ref, moved_ref):
    kept_ref[...] = own_ref[:KEPT]
    moved_ref[: own_ref.shape[0] - KEPT] = own_ref[KEPT:]
    names = groups_ref[...].astype(jnp.float32)
    moved_ref[own_ref.shape[0] - KEPT :] = jnp.broadcast_to(names, (16, names.shape[1])).astype(
        moved_ref.dtype
    )


def split(groups, own):
    tokens, channels = own.shape
    return pl.pallas_call(
        split_kernel,
        out_shape=[
            jax.ShapeDtypeStruct((KEPT, channels), own.dtype),
            jax.ShapeDtypeStruct((tokens - KEPT + 16, channels), own.dtype),
        ],
        compiler_params=pltpu.CompilerParams(vmem_limit_bytes=VMEM_LIMIT),
    )(groups, own)


def square_kernel(start, named, groups_ref, own_ref, *refs):
    count = refs[-1].shape[1]
    total = own_ref[start : start + count].astype(jnp.float32)
    groups = groups_ref[...]
    if len(refs) == 2:
        total = total + refs[0][:count].astype(jnp.float32)
        if named:
            groups = refs[0][count:].astype(jnp.float32).astype(jnp.int32)
    group = lax.broadcasted_iota(jnp.int32, (16, groups_ref.shape[1]), 0)
    onehot = jnp.where(groups == group, 1.0, 0.0).astype(jnp.bfloat16)
    rest = total * total
    result = jnp.zeros((16, count), jnp.float32)
    for _ in range(3):
        part = rest.astype(jnp.bfloat16)
        rest = rest - part.astype(jnp.float32)
        result += lax.dot_general(
            onehot, part, (((1,), (1,)), ((), ())), preferred_element_type=jnp.float32
        )
    refs[-1][...] = result[:GROUPS]


def group_squares(groups, own, start, stop, *other, named=False):
    return pl.pallas_call(
        functools.partial(square_kernel, start, named),
        out_shape=jax.ShapeDtypeStruct((GROUPS, stop - start), jnp.float32),
        compiler_params=pltpu.CompilerParams(vmem_limit_bytes=VMEM_LIMIT),
    )(groups, own, *other)


def section_weights(own, groups, meanwhile):
    tokens = own.shape[0]
    kept, moved = split(groups, own)
    first = lax.ppermute(moved, "section", [(0, 1)])
    later = lax.ppermute(kept, "section", [(1, 0)])
    alone = group_squares(groups, own, KEPT, tokens)
    first, alone, *meanwhile = lax.optimization_barrier((first, alone, *meanwhile))
    back = group_squares(groups, own, KEPT, tokens, first, named=True)
    back = lax.ppermute(back, "section", [(1, 0)])
    rest = jnp.where(lax.axis_index("section") == 0, back, alone)
    partial = jnp.concatenate([group_squares(groups, own, 0, KEPT, later), rest], 1)
    count = lax.axis_size("tensor")
    partial += lax.ppermute(partial, "tensor", [(i, i ^ 1) for i in range(count)])
    chips = [list(range(core, count, 2)) for core in (0, 1)]
    spread = jnp.broadcast_to(partial[None], (count // 2, GROUPS, tokens))
    spread = lax.all_to_all(spread, "tensor", 0, 0, axis_index_groups=chips, tiled=True)
    return spread.sum(0) / D, *meanwhile


def pair_tiles(mean, out_ref, at):
    count = mean.shape[0]
    whole = mean.shape[1] // LANES
    for c in range(whole):
        out_ref[at + c * count : at + (c + 1) * count] = mean[:, c * LANES : (c + 1) * LANES]
    rest = mean[:, whole * LANES :]
    at += whole * count
    out_ref[at : at + count // 2] = jnp.concatenate([rest[: count // 2], rest[count // 2 :]], 1)


def dot(left, right):
    return lax.dot_general(
        left, right, (((1,), (1,)), ((), ())), preferred_element_type=jnp.float32
    )


def mean_of_orders(one, two, scaled_one, scaled_two):
    count = one.shape[0]
    other = dot(jnp.concatenate(scaled_one, 0), two)
    other = [other[g * count : (g + 1) * count] for g in range(GROUPS)]
    return 0.5 * (dot(one, jnp.concatenate(scaled_two, 0)) + jnp.concatenate(other, 1))


def first_kernel(one, two, weight_ref, turned_ref, peak_ref, top_ref, out_ref):
    most = weight_ref[...] * (peak_ref[...] * peak_ref[...])
    most = jnp.max(jnp.max(most, axis=0, keepdims=True), axis=1, keepdims=True)
    most = jnp.ceil(jnp.log2(jnp.maximum(most, 1e-30)))
    top_ref[...] = jnp.broadcast_to(most, top_ref.shape)
    count = turned_ref.shape[0] // DP
    rows, scaled = [], []
    for b in (one, two):
        rows.append(turned_ref[b * count : (b + 1) * count])
        wide = rows[-1].astype(jnp.float32)
        scaled.append(
            [(wide * weight_ref[g : g + 1]).astype(jnp.bfloat16) for g in range(GROUPS)]
        )
    pair_tiles(mean_of_orders(*rows, *scaled), out_ref, 0)


def first_sums(weight, turned, peak, one, two, shape):
    return pl.pallas_call(
        functools.partial(first_kernel, one, two),
        out_shape=[
            jax.ShapeDtypeStruct((8, LANES), jnp.float32),
            jax.ShapeDtypeStruct((shape, LANES), jnp.float32),
        ],
        compiler_params=pltpu.CompilerParams(vmem_limit_bytes=PRODUCT_VMEM_LIMIT),
        cost_estimate=pl.CostEstimate(flops=1, bytes_accessed=1, transcendentals=0),
    )(weight, turned, peak)


def product_kernel(make, table_ref, factors_ref, turned_ref, *refs):
    out_ref = refs[-1]
    scaled_ref = refs[0] if make else factors_ref
    count = turned_ref.shape[0] // DP
    tiles = DP * count // LANES

    def place(b):
        return pl.ds(pl.multiple_of(lax.rem(b, DP) * count, 16), count)

    def scale(b, carry):
        rows = turned_ref[place(b)].astype(jnp.float32)
        for g in range(GROUPS):
            scaled_ref[g, place(b)] = (rows * factors_ref[g : g + 1]).astype(jnp.bfloat16)
        return carry

    def work(job, carry):
        block, half, one, two = (table_ref[job, n] for n in range(4))
        right = [scaled_ref[2 * half + q, place(block + c)] for q in (0, 1) for c in OWN]
        result = dot(turned_ref[place(block)], jnp.concatenate(right, 0))
        for c in range(tiles):
            out_ref[job, c * count : (c + 1) * count] = result[:, c * LANES : (c + 1) * LANES]
        mean = mean_of_orders(
            turned_ref[place(one)],
            turned_ref[place(two)],
            [scaled_ref[g, place(one)] for g in range(GROUPS)],
            [scaled_ref[g, place(two)] for g in range(GROUPS)],
        )
        pair_tiles(mean, out_ref.at[job], tiles * count)
        return carry

    if make:
        lax.fori_loop(0, DP, scale, 0)
    lax.fori_loop(0, out_ref.shape[0], work, 0, unroll=2)


def products(factors, turned, shape, jobs):
    make = factors.ndim == 2
    table = jnp.array([[b % DP, half, x % DP, y % DP] for b, half, x, y in jobs], jnp.int32)
    out_shape = [jax.ShapeDtypeStruct((len(jobs), shape, LANES), jnp.float32)]
    if make:
        out_shape.insert(0, jax.ShapeDtypeStruct((GROUPS, *turned.shape), jnp.bfloat16))
    vmem = pl.BlockSpec(memory_space=pltpu.VMEM)
    return pl.pallas_call(
        functools.partial(product_kernel, make),
        in_specs=[pl.BlockSpec(memory_space=pltpu.SMEM), vmem, vmem],
        out_specs=[vmem] * len(out_shape),
        out_shape=out_shape,
        compiler_params=pltpu.CompilerParams(vmem_limit_bytes=PRODUCT_VMEM_LIMIT),
        cost_estimate=pl.CostEstimate(flops=1, bytes_accessed=1, transcendentals=0),
    )(table, factors, turned)


def finish_kernel(factor, me_ref, *refs):
    *sums_refs, out_ref = refs
    own_refs, one_refs, two_refs, got_refs = (sums_refs[n : n + 2] for n in (0, 2, 4, 6))
    count = out_ref.shape[0]
    size = own_refs[0].shape[0]
    width = DP * count
    whole = GROUPS * count // LANES

    def pair(ref, got_ref, at):
        def rows(start, stop):
            return ref[start:stop] + got_ref[at + start : at + stop]

        parts = [rows(c * count, (c + 1) * count) for c in range(whole)]
        rest = rows(whole * count, whole * count + count // 2)
        rest = jnp.concatenate([rest[:, : LANES // 2], rest[:, LANES // 2 :]], 0)
        return jnp.concatenate([*parts, rest], 1)

    both = [(side, 1 - side) for side in (0, 1)]
    ones = [pair(one_refs[i], got_refs[j], size + one_refs[i].shape[0]) for i, j in both]
    twos = [pair(two_refs[i], got_refs[j], size) for i, j in both]
    for p in (0, 1):
        parts = []
        for at in range(0, size, count):
            parts.append(own_refs[p][at : at + count] + got_refs[p][at : at + count])
        own = jnp.concatenate(parts, 1)
        for q in (0, 1):
            g = 2 * p + q
            blocks = [None] * DP
            for n, c in enumerate(OWN):
                at = (q * len(OWN) + n) * count
                blocks[c] = own[:, at : at + count]
            group = slice(g * count, (g + 1) * count)
            blocks[1], blocks[2] = ones[0][:, group], twos[0][:, group]
            blocks[7], blocks[6] = ones[1][:, group].T, twos[1][:, group].T
            row = jnp.concatenate(blocks, 1)
            row = pltpu.roll(row, me_ref[0] * count, 1)
            out_ref[:, g * width : (g + 1) * width] = row * factor


def finish(me, own, ones, twos, got, count, factor):
    vmem = pl.BlockSpec(memory_space=pltpu.VMEM)
    return pl.pallas_call(
        functools.partial(finish_kernel, factor),
        in_specs=[pl.BlockSpec(memory_space=pltpu.SMEM)] + [vmem] * 8,
        out_specs=vmem,
        out_shape=jax.ShapeDtypeStruct((count, GROUPS * DP * count), jnp.float32),
        compiler_params=pltpu.CompilerParams(vmem_limit_bytes=PRODUCT_VMEM_LIMIT),
    )(me, *own, *ones, *twos, *got)


def on_device(grads, groups, acts):
    me = lax.axis_index("dp").astype(jnp.int32)
    cols = acts[0]
    tokens, width = cols.shape
    rows = width // DP
    turned = cols.T
    peak = jnp.max(jnp.abs(turned), axis=0, keepdims=True).astype(jnp.float32)
    turned = lax.dynamic_slice_in_dim(jnp.concatenate([turned, turned], 0), me * rows, width, 0)
    weight, turned, peak = section_weights(grads[0], groups, (turned, peak))

    size = width // LANES * rows
    pair = GROUPS * rows * rows // LANES
    long, short = size + pair + 8, pair + 8

    top, ahead0 = first_sums(weight, turned, peak, 3, 5, short)
    top = top[:1]
    way, both = (1, -1), (0, 1)
    scaled, begin = products(weight, turned, long, [(3, 1, 3, 4), (5, 0, 4, 5)])
    sums = {(2, 0): begin[0], (2, 1): begin[1]}
    bits = 15 - (tokens * DP - 1).bit_length()

    def pack(value, level):
        room = lax.broadcasted_iota(jnp.int32, value.shape, 0) >= value.shape[0] - 8
        return jnp.where(room, level, value * jnp.exp2(bits - level)).astype(SENT)

    def tag_of(value):
        return value[-1:].astype(jnp.float32)

    def unpack(value):
        return value.astype(jnp.float32) * jnp.exp2(tag_of(value) - bits)

    def send(packed):
        return [shift(packed[i], "dp", way[i]) for i in both]

    start = shift(pack(ahead0, top), "dp", 1)
    got, sent = {}, {}
    sent[2] = [pack(sums[2, i], top) for i in both]
    got[2] = send(sent[2])

    def later(*steps):
        nonlocal scaled
        scaled = lax.optimization_barrier((scaled, *(v for pair in sent.values() for v in pair)))[0]
        jobs = []
        for k in steps:
            ahead, behind, distance = (2 - k // 2, k // 2 - 4, 2) if k % 2 else (4 - k // 2, k // 2 - 5, 1)
            block = (8 - k) // 2 + k % 2
            for i, one in enumerate((ahead, behind)):
                half = i if k == 8 else (k + 1 + i) % 2
                jobs.append((block * way[i], half, one, one + distance))
        result = products(scaled, turned, long, jobs)[0]
        for n, k in enumerate(steps):
            for i in both:
                sums[k, i] = result[2 * n + i]
        return [result]

    def tie(k, *others):
        got[k] = lax.optimization_barrier((*got[k], *others))[:2]

    later(1)
    begun = jnp.pad(unpack(start)[:pair], ((size, 8), (0, 0)))
    sent[1] = [pack(sums[1, 0] + begun, jnp.maximum(top, tag_of(start))), pack(sums[1, 1], top)]
    got[1] = send(sent[1])
    tie(2, *later(3, 4))
    kept = {}
    for k in (4, 3, 6, 5, 7):
        before = [unpack(got[k - 2][i]) for i in both]
        value = [sums[k, i] + before[i] for i in both]
        level = [jnp.maximum(top, tag_of(got[k - 2][i])) for i in both]
        if k == 5:
            kept[2] = [v[size : size + pair] for v in value]
        if k == 7:
            even = [unpack(got[6][i]) for i in both]
            kept[1] = [(sums[8, i] + even[i])[size : size + pair] for i in both]
            own = [sums[8, i][:size] + even[1 - i][:size] for i in both]
            level = [jnp.maximum(level[i], tag_of(got[6][i])) for i in both]
            room = jnp.zeros((16, LANES), jnp.float32)
            value = [jnp.concatenate([value[i][:-8], kept[1][i], room], 0) for i in both]
        sent[k] = [pack(value[i], level[i]) for i in both]
        got[k] = send(sent[k])
        if k == 4:
            tie(1, *later(5, 6))
        elif k == 3:
            tie(4, *later(7, 8))
        elif k < 7:
            tie(9 - k if k == 6 else k + 1, *sent[k])

    factor = 1.0 / (tokens * DP)
    end = [unpack(got[7][i]) for i in both]
    return finish(me.reshape(1), own, kept[1], kept[2], end, rows, factor)[None]


def solution(mesh):
    return jax.shard_map(
        on_device,
        mesh=mesh,
        in_specs=(
            P("section", "dp", "tensor"),
            P("section", "tensor"),
            P("section", "dp", "tensor"),
        ),
        out_specs=P("section", ("tensor", "dp"), None),
        check_vma=False,
    )
```

```python
import functools

import jax
import jax.numpy as jnp
from jax import lax
from jax.experimental import pallas as pl
from jax.experimental.pallas import tpu as pltpu
from jax.sharding import PartitionSpec as P

D = 8192
GROUPS = 4
DP = 8
LANES = 128
OWN = (0, 3, 4, 5)
SENT = jnp.float16
VMEM_LIMIT = 8 * 1024 * 1024
PRODUCT_VMEM_LIMIT = 24 * 1024 * 1024
KEPT = 576


def shift(value, axis, steps):
    count = lax.axis_size(axis)
    return lax.ppermute(value, axis, [(i, (i + steps) % count) for i in range(count)])


def split_kernel(groups_ref, own_ref, kept_ref, moved_ref):
    kept_ref[...] = own_ref[:KEPT]
    moved_ref[: own_ref.shape[0] - KEPT] = own_ref[KEPT:]
    names = groups_ref[...].astype(jnp.float32)
    moved_ref[own_ref.shape[0] - KEPT :] = jnp.broadcast_to(names, (16, names.shape[1])).astype(
        moved_ref.dtype
    )


def split(groups, own):
    tokens, channels = own.shape
    return pl.pallas_call(
        split_kernel,
        out_shape=[
            jax.ShapeDtypeStruct((KEPT, channels), own.dtype),
            jax.ShapeDtypeStruct((tokens - KEPT + 16, channels), own.dtype),
        ],
        compiler_params=pltpu.CompilerParams(vmem_limit_bytes=VMEM_LIMIT),
    )(groups, own)


def square_kernel(start, named, groups_ref, own_ref, *refs):
    count = refs[-1].shape[1]
    total = own_ref[start : start + count].astype(jnp.float32)
    groups = groups_ref[...]
    if len(refs) == 2:
        total = total + refs[0][:count].astype(jnp.float32)
        if named:
            groups = refs[0][count:].astype(jnp.float32).astype(jnp.int32)
    group = lax.broadcasted_iota(jnp.int32, (16, groups_ref.shape[1]), 0)
    onehot = jnp.where(groups == group, 1.0, 0.0).astype(jnp.bfloat16)
    rest = total * total
    result = jnp.zeros((16, count), jnp.float32)
    for _ in range(3):
        part = rest.astype(jnp.bfloat16)
        rest = rest - part.astype(jnp.float32)
        result += lax.dot_general(
            onehot, part, (((1,), (1,)), ((), ())), preferred_element_type=jnp.float32
        )
    refs[-1][...] = result[:GROUPS]


def group_squares(groups, own, start, stop, *other, named=False):
    return pl.pallas_call(
        functools.partial(square_kernel, start, named),
        out_shape=jax.ShapeDtypeStruct((GROUPS, stop - start), jnp.float32),
        compiler_params=pltpu.CompilerParams(vmem_limit_bytes=VMEM_LIMIT),
    )(groups, own, *other)


def section_weights(own, groups, meanwhile):
    tokens = own.shape[0]
    kept, moved = split(groups, own)
    first = lax.ppermute(moved, "section", [(0, 1)])
    later = lax.ppermute(kept, "section", [(1, 0)])
    alone = group_squares(groups, own, KEPT, tokens)
    first, alone, *meanwhile = lax.optimization_barrier((first, alone, *meanwhile))
    back = group_squares(groups, own, KEPT, tokens, first, named=True)
    back = lax.ppermute(back, "section", [(1, 0)])
    rest = jnp.where(lax.axis_index("section") == 0, back, alone)
    partial = jnp.concatenate([group_squares(groups, own, 0, KEPT, later), rest], 1)
    count = lax.axis_size("tensor")
    partial += lax.ppermute(partial, "tensor", [(i, i ^ 1) for i in range(count)])
    chips = [list(range(core, count, 2)) for core in (0, 1)]
    spread = jnp.broadcast_to(partial[None], (count // 2, GROUPS, tokens))
    spread = lax.all_to_all(spread, "tensor", 0, 0, axis_index_groups=chips, tiled=True)
    return spread.sum(0) / D, *meanwhile


def pair_tiles(mean, out_ref, at):
    count = mean.shape[0]
    whole = mean.shape[1] // LANES
    for c in range(whole):
        out_ref[at + c * count : at + (c + 1) * count] = mean[:, c * LANES : (c + 1) * LANES]
    rest = mean[:, whole * LANES :]
    at += whole * count
    out_ref[at : at + count // 2] = jnp.concatenate([rest[: count // 2], rest[count // 2 :]], 1)


def dot(left, right):
    return lax.dot_general(
        left, right, (((1,), (1,)), ((), ())), preferred_element_type=jnp.float32
    )


def mean_of_orders(one, two, scaled_one, scaled_two):
    count = one.shape[0]
    other = dot(jnp.concatenate(scaled_one, 0), two)
    other = [other[g * count : (g + 1) * count] for g in range(GROUPS)]
    return 0.5 * (dot(one, jnp.concatenate(scaled_two, 0)) + jnp.concatenate(other, 1))


def first_kernel(one, two, weight_ref, turned_ref, peak_ref, top_ref, out_ref):
    most = weight_ref[...] * (peak_ref[...] * peak_ref[...])
    most = jnp.max(jnp.max(most, axis=0, keepdims=True), axis=1, keepdims=True)
    most = jnp.ceil(jnp.log2(jnp.maximum(most, 1e-30)))
    top_ref[...] = jnp.broadcast_to(most, top_ref.shape)
    count = turned_ref.shape[0] // DP
    rows, scaled = [], []
    for b in (one, two):
        rows.append(turned_ref[b * count : (b + 1) * count])
        wide = rows[-1].astype(jnp.float32)
        scaled.append(
            [(wide * weight_ref[g : g + 1]).astype(jnp.bfloat16) for g in range(GROUPS)]
        )
    pair_tiles(mean_of_orders(*rows, *scaled), out_ref, 0)


def first_sums(weight, turned, peak, one, two, shape):
    return pl.pallas_call(
        functools.partial(first_kernel, one, two),
        out_shape=[
            jax.ShapeDtypeStruct((8, LANES), jnp.float32),
            jax.ShapeDtypeStruct((shape, LANES), jnp.float32),
        ],
        compiler_params=pltpu.CompilerParams(vmem_limit_bytes=PRODUCT_VMEM_LIMIT),
        cost_estimate=pl.CostEstimate(flops=1, bytes_accessed=1, transcendentals=0),
    )(weight, turned, peak)


def product_kernel(make, table_ref, factors_ref, turned_ref, *refs):
    out_ref = refs[-1]
    scaled_ref = refs[0] if make else factors_ref
    count = turned_ref.shape[0] // DP
    tiles = DP * count // LANES

    def place(b):
        return pl.ds(pl.multiple_of(lax.rem(b, DP) * count, 16), count)

    def scale(b, carry):
        rows = turned_ref[place(b)].astype(jnp.float32)
        for g in range(GROUPS):
            scaled_ref[g, place(b)] = (rows * factors_ref[g : g + 1]).astype(jnp.bfloat16)
        return carry

    def work(job, carry):
        block, half, one, two = (table_ref[job, n] for n in range(4))
        right = [scaled_ref[2 * half + q, place(block + c)] for q in (0, 1) for c in OWN]
        result = dot(turned_ref[place(block)], jnp.concatenate(right, 0))
        for c in range(tiles):
            out_ref[job, c * count : (c + 1) * count] = result[:, c * LANES : (c + 1) * LANES]
        mean = mean_of_orders(
            turned_ref[place(one)],
            turned_ref[place(two)],
            [scaled_ref[g, place(one)] for g in range(GROUPS)],
            [scaled_ref[g, place(two)] for g in range(GROUPS)],
        )
        pair_tiles(mean, out_ref.at[job], tiles * count)
        return carry

    if make:
        lax.fori_loop(0, DP, scale, 0)
    lax.fori_loop(0, out_ref.shape[0], work, 0, unroll=2)


def products(factors, turned, shape, jobs):
    make = factors.ndim == 2
    table = jnp.array([[b % DP, half, x % DP, y % DP] for b, half, x, y in jobs], jnp.int32)
    out_shape = [jax.ShapeDtypeStruct((len(jobs), shape, LANES), jnp.float32)]
    if make:
        out_shape.insert(0, jax.ShapeDtypeStruct((GROUPS, *turned.shape), jnp.bfloat16))
    vmem = pl.BlockSpec(memory_space=pltpu.VMEM)
    return pl.pallas_call(
        functools.partial(product_kernel, make),
        in_specs=[pl.BlockSpec(memory_space=pltpu.SMEM), vmem, vmem],
        out_specs=[vmem] * len(out_shape),
        out_shape=out_shape,
        compiler_params=pltpu.CompilerParams(vmem_limit_bytes=PRODUCT_VMEM_LIMIT),
        cost_estimate=pl.CostEstimate(flops=1, bytes_accessed=1, transcendentals=0),
    )(table, factors, turned)


def finish_kernel(factor, me_ref, *refs):
    *sums_refs, out_ref = refs
    own_refs, one_refs, two_refs, got_refs = (sums_refs[n : n + 2] for n in (0, 2, 4, 6))
    count = out_ref.shape[0]
    size = own_refs[0].shape[0]
    width = DP * count
    whole = GROUPS * count // LANES

    def pair(ref, got_ref, at):
        def rows(start, stop):
            return ref[start:stop] + got_ref[at + start : at + stop]

        parts = [rows(c * count, (c + 1) * count) for c in range(whole)]
        rest = rows(whole * count, whole * count + count // 2)
        rest = jnp.concatenate([rest[:, : LANES // 2], rest[:, LANES // 2 :]], 0)
        return jnp.concatenate([*parts, rest], 1)

    both = [(side, 1 - side) for side in (0, 1)]
    ones = [pair(one_refs[i], got_refs[j], size + one_refs[i].shape[0]) for i, j in both]
    twos = [pair(two_refs[i], got_refs[j], size) for i, j in both]
    for p in (0, 1):
        parts = []
        for at in range(0, size, count):
            parts.append(own_refs[p][at : at + count] + got_refs[p][at : at + count])
        own = jnp.concatenate(parts, 1)
        for q in (0, 1):
            g = 2 * p + q
            blocks = [None] * DP
            for n, c in enumerate(OWN):
                at = (q * len(OWN) + n) * count
                blocks[c] = own[:, at : at + count]
            group = slice(g * count, (g + 1) * count)
            blocks[1], blocks[2] = ones[0][:, group], twos[0][:, group]
            blocks[7], blocks[6] = ones[1][:, group].T, twos[1][:, group].T
            row = jnp.concatenate(blocks, 1)
            row = pltpu.roll(row, me_ref[0] * count, 1)
            out_ref[:, g * width : (g + 1) * width] = row * factor


def finish(me, own, ones, twos, got, count, factor):
    vmem = pl.BlockSpec(memory_space=pltpu.VMEM)
    return pl.pallas_call(
        functools.partial(finish_kernel, factor),
        in_specs=[pl.BlockSpec(memory_space=pltpu.SMEM)] + [vmem] * 8,
        out_specs=vmem,
        out_shape=jax.ShapeDtypeStruct((count, GROUPS * DP * count), jnp.float32),
        compiler_params=pltpu.CompilerParams(vmem_limit_bytes=PRODUCT_VMEM_LIMIT),
    )(me, *own, *ones, *twos, *got)


def on_device(grads, groups, acts):
    me = lax.axis_index("dp").astype(jnp.int32)
    cols = acts[0]
    tokens, width = cols.shape
    rows = width // DP
    turned = cols.T
    peak = jnp.max(jnp.abs(turned), axis=0, keepdims=True).astype(jnp.float32)
    turned = lax.dynamic_slice_in_dim(jnp.concatenate([turned, turned], 0), me * rows, width, 0)
    weight, turned, peak = section_weights(grads[0], groups, (turned, peak))

    size = width // LANES * rows
    pair = GROUPS * rows * rows // LANES
    long, short = size + pair + 8, pair + 8

    top, ahead0 = first_sums(weight, turned, peak, 3, 5, short)
    top = top[:1]
    way, both = (1, -1), (0, 1)
    scaled, begin = products(weight, turned, long, [(3, 1, 3, 4), (5, 0, 4, 5)])
    sums = {(2, 0): begin[0], (2, 1): begin[1]}
    bits = 15 - (tokens * DP - 1).bit_length()

    def pack(value, level):
        room = lax.broadcasted_iota(jnp.int32, value.shape, 0) >= value.shape[0] - 8
        return jnp.where(room, level, value * jnp.exp2(bits - level)).astype(SENT)

    def tag_of(value):
        return value[-1:].astype(jnp.float32)

    def unpack(value):
        return value.astype(jnp.float32) * jnp.exp2(tag_of(value) - bits)

    def send(packed):
        return [shift(packed[i], "dp", way[i]) for i in both]

    start = shift(pack(ahead0, top), "dp", 1)
    got, sent = {}, {}
    sent[2] = [pack(sums[2, i], top) for i in both]
    got[2] = send(sent[2])

    def later(*steps):
        nonlocal scaled
        scaled = lax.optimization_barrier((scaled, *(v for pair in sent.values() for v in pair)))[0]
        jobs = []
        for k in steps:
            ahead, behind, distance = (2 - k // 2, k // 2 - 4, 2) if k % 2 else (4 - k // 2, k // 2 - 5, 1)
            block = (8 - k) // 2 + k % 2
            for i, one in enumerate((ahead, behind)):
                half = i if k == 8 else (k + 1 + i) % 2
                jobs.append((block * way[i], half, one, one + distance))
        result = products(scaled, turned, long, jobs)[0]
        for n, k in enumerate(steps):
            for i in both:
                sums[k, i] = result[2 * n + i]
        return [result]

    def tie(k, *others):
        got[k] = lax.optimization_barrier((*got[k], *others))[:2]

    later(1)
    begun = jnp.pad(unpack(start)[:pair], ((size, 8), (0, 0)))
    sent[1] = [pack(sums[1, 0] + begun, jnp.maximum(top, tag_of(start))), pack(sums[1, 1], top)]
    got[1] = send(sent[1])
    tie(2, *later(3, 4))
    kept = {}
    for k in (4, 3, 6, 5, 7):
        before = [unpack(got[k - 2][i]) for i in both]
        value = [sums[k, i] + before[i] for i in both]
        level = [jnp.maximum(top, tag_of(got[k - 2][i])) for i in both]
        if k == 5:
            kept[2] = [v[size : size + pair] for v in value]
        if k == 7:
            even = [unpack(got[6][i]) for i in both]
            kept[1] = [(sums[8, i] + even[i])[size : size + pair] for i in both]
            own = [sums[8, i][:size] + even[1 - i][:size] for i in both]
            level = [jnp.maximum(level[i], tag_of(got[6][i])) for i in both]
            room = jnp.zeros((16, LANES), jnp.float32)
            value = [jnp.concatenate([value[i][:-8], kept[1][i], room], 0) for i in both]
        sent[k] = [pack(value[i], level[i]) for i in both]
        got[k] = send(sent[k])
        if k == 4:
            tie(1, *sent[k])
        elif k == 3:
            tie(4, *later(5, 6))
        elif k == 6:
            tie(3, *later(7, 8))
        elif k < 7:
            tie(9 - k if k == 6 else k + 1, *sent[k])

    factor = 1.0 / (tokens * DP)
    end = [unpack(got[7][i]) for i in both]
    return finish(me.reshape(1), own, kept[1], kept[2], end, rows, factor)[None]


def solution(mesh):
    return jax.shard_map(
        on_device,
        mesh=mesh,
        in_specs=(
            P("section", "dp", "tensor"),
            P("section", "tensor"),
            P("section", "dp", "tensor"),
        ),
        out_specs=P("section", ("tensor", "dp"), None),
        check_vma=False,
    )
```

```python
import functools

import jax
import jax.numpy as jnp
from jax import lax
from jax.experimental import pallas as pl
from jax.experimental.pallas import tpu as pltpu
from jax.sharding import PartitionSpec as P

D = 8192
GROUPS = 4
DP = 8
LANES = 128
OWN = (0, 3, 4, 5)
SENT = jnp.float16
VMEM_LIMIT = 8 * 1024 * 1024
PRODUCT_VMEM_LIMIT = 24 * 1024 * 1024
KEPT = 608


def shift(value, axis, steps):
    count = lax.axis_size(axis)
    return lax.ppermute(value, axis, [(i, (i + steps) % count) for i in range(count)])


def split_kernel(groups_ref, own_ref, kept_ref, moved_ref):
    kept_ref[...] = own_ref[:KEPT]
    moved_ref[: own_ref.shape[0] - KEPT] = own_ref[KEPT:]
    names = groups_ref[...].astype(jnp.float32)
    moved_ref[own_ref.shape[0] - KEPT :] = jnp.broadcast_to(names, (16, names.shape[1])).astype(
        moved_ref.dtype
    )


def split(groups, own):
    tokens, channels = own.shape
    return pl.pallas_call(
        split_kernel,
        out_shape=[
            jax.ShapeDtypeStruct((KEPT, channels), own.dtype),
            jax.ShapeDtypeStruct((tokens - KEPT + 16, channels), own.dtype),
        ],
        compiler_params=pltpu.CompilerParams(vmem_limit_bytes=VMEM_LIMIT),
    )(groups, own)


def square_kernel(start, named, groups_ref, own_ref, *refs):
    count = refs[-1].shape[1]
    total = own_ref[start : start + count].astype(jnp.float32)
    groups = groups_ref[...]
    if len(refs) == 2:
        total = total + refs[0][:count].astype(jnp.float32)
        if named:
            groups = refs[0][count:].astype(jnp.float32).astype(jnp.int32)
    group = lax.broadcasted_iota(jnp.int32, (16, groups_ref.shape[1]), 0)
    onehot = jnp.where(groups == group, 1.0, 0.0).astype(jnp.bfloat16)
    rest = total * total
    result = jnp.zeros((16, count), jnp.float32)
    for _ in range(3):
        part = rest.astype(jnp.bfloat16)
        rest = rest - part.astype(jnp.float32)
        result += lax.dot_general(
            onehot, part, (((1,), (1,)), ((), ())), preferred_element_type=jnp.float32
        )
    refs[-1][...] = result[:GROUPS]


def group_squares(groups, own, start, stop, *other, named=False):
    return pl.pallas_call(
        functools.partial(square_kernel, start, named),
        out_shape=jax.ShapeDtypeStruct((GROUPS, stop - start), jnp.float32),
        compiler_params=pltpu.CompilerParams(vmem_limit_bytes=VMEM_LIMIT),
    )(groups, own, *other)


def section_weights(own, groups, meanwhile):
    tokens = own.shape[0]
    kept, moved = split(groups, own)
    first = lax.ppermute(moved, "section", [(0, 1)])
    later = lax.ppermute(kept, "section", [(1, 0)])
    alone = group_squares(groups, own, KEPT, tokens)
    first, alone, *meanwhile = lax.optimization_barrier((first, alone, *meanwhile))
    back = group_squares(groups, own, KEPT, tokens, first, named=True)
    back = lax.ppermute(back, "section", [(1, 0)])
    rest = jnp.where(lax.axis_index("section") == 0, back, alone)
    partial = jnp.concatenate([group_squares(groups, own, 0, KEPT, later), rest], 1)
    count = lax.axis_size("tensor")
    partial += lax.ppermute(partial, "tensor", [(i, i ^ 1) for i in range(count)])
    chips = [list(range(core, count, 2)) for core in (0, 1)]
    spread = jnp.broadcast_to(partial[None], (count // 2, GROUPS, tokens))
    spread = lax.all_to_all(spread, "tensor", 0, 0, axis_index_groups=chips, tiled=True)
    return spread.sum(0) / D, *meanwhile


def pair_tiles(mean, out_ref, at):
    count = mean.shape[0]
    whole = mean.shape[1] // LANES
    for c in range(whole):
        out_ref[at + c * count : at + (c + 1) * count] = mean[:, c * LANES : (c + 1) * LANES]
    rest = mean[:, whole * LANES :]
    at += whole * count
    out_ref[at : at + count // 2] = jnp.concatenate([rest[: count // 2], rest[count // 2 :]], 1)


def dot(left, right):
    return lax.dot_general(
        left, right, (((1,), (1,)), ((), ())), preferred_element_type=jnp.float32
    )


def mean_of_orders(one, two, scaled_one, scaled_two):
    count = one.shape[0]
    other = dot(jnp.concatenate(scaled_one, 0), two)
    other = [other[g * count : (g + 1) * count] for g in range(GROUPS)]
    return 0.5 * (dot(one, jnp.concatenate(scaled_two, 0)) + jnp.concatenate(other, 1))


def first_kernel(one, two, weight_ref, turned_ref, peak_ref, top_ref, out_ref):
    most = weight_ref[...] * (peak_ref[...] * peak_ref[...])
    most = jnp.max(jnp.max(most, axis=0, keepdims=True), axis=1, keepdims=True)
    most = jnp.ceil(jnp.log2(jnp.maximum(most, 1e-30)))
    top_ref[...] = jnp.broadcast_to(most, top_ref.shape)
    count = turned_ref.shape[0] // DP
    rows, scaled = [], []
    for b in (one, two):
        rows.append(turned_ref[b * count : (b + 1) * count])
        wide = rows[-1].astype(jnp.float32)
        scaled.append(
            [(wide * weight_ref[g : g + 1]).astype(jnp.bfloat16) for g in range(GROUPS)]
        )
    pair_tiles(mean_of_orders(*rows, *scaled), out_ref, 0)


def first_sums(weight, turned, peak, one, two, shape):
    return pl.pallas_call(
        functools.partial(first_kernel, one, two),
        out_shape=[
            jax.ShapeDtypeStruct((8, LANES), jnp.float32),
            jax.ShapeDtypeStruct((shape, LANES), jnp.float32),
        ],
        compiler_params=pltpu.CompilerParams(vmem_limit_bytes=PRODUCT_VMEM_LIMIT),
        cost_estimate=pl.CostEstimate(flops=1, bytes_accessed=1, transcendentals=0),
    )(weight, turned, peak)


def product_kernel(make, table_ref, factors_ref, turned_ref, *refs):
    out_ref = refs[-1]
    scaled_ref = refs[0] if make else factors_ref
    count = turned_ref.shape[0] // DP
    tiles = DP * count // LANES

    def place(b):
        return pl.ds(pl.multiple_of(lax.rem(b, DP) * count, 16), count)

    def scale(b, carry):
        rows = turned_ref[place(b)].astype(jnp.float32)
        for g in range(GROUPS):
            scaled_ref[g, place(b)] = (rows * factors_ref[g : g + 1]).astype(jnp.bfloat16)
        return carry

    def work(job, carry):
        block, half, one, two = (table_ref[job, n] for n in range(4))
        right = [scaled_ref[2 * half + q, place(block + c)] for q in (0, 1) for c in OWN]
        result = dot(turned_ref[place(block)], jnp.concatenate(right, 0))
        for c in range(tiles):
            out_ref[job, c * count : (c + 1) * count] = result[:, c * LANES : (c + 1) * LANES]
        mean = mean_of_orders(
            turned_ref[place(one)],
            turned_ref[place(two)],
            [scaled_ref[g, place(one)] for g in range(GROUPS)],
            [scaled_ref[g, place(two)] for g in range(GROUPS)],
        )
        pair_tiles(mean, out_ref.at[job], tiles * count)
        return carry

    if make:
        lax.fori_loop(0, DP, scale, 0)
    lax.fori_loop(0, out_ref.shape[0], work, 0, unroll=2)


def products(factors, turned, shape, jobs):
    make = factors.ndim == 2
    table = jnp.array([[b % DP, half, x % DP, y % DP] for b, half, x, y in jobs], jnp.int32)
    out_shape = [jax.ShapeDtypeStruct((len(jobs), shape, LANES), jnp.float32)]
    if make:
        out_shape.insert(0, jax.ShapeDtypeStruct((GROUPS, *turned.shape), jnp.bfloat16))
    vmem = pl.BlockSpec(memory_space=pltpu.VMEM)
    return pl.pallas_call(
        functools.partial(product_kernel, make),
        in_specs=[pl.BlockSpec(memory_space=pltpu.SMEM), vmem, vmem],
        out_specs=[vmem] * len(out_shape),
        out_shape=out_shape,
        compiler_params=pltpu.CompilerParams(vmem_limit_bytes=PRODUCT_VMEM_LIMIT),
        cost_estimate=pl.CostEstimate(flops=1, bytes_accessed=1, transcendentals=0),
    )(table, factors, turned)


def finish_kernel(factor, me_ref, *refs):
    *sums_refs, out_ref = refs
    own_refs, one_refs, two_refs, got_refs = (sums_refs[n : n + 2] for n in (0, 2, 4, 6))
    count = out_ref.shape[0]
    size = own_refs[0].shape[0]
    width = DP * count
    whole = GROUPS * count // LANES

    def pair(ref, got_ref, at):
        def rows(start, stop):
            return ref[start:stop] + got_ref[at + start : at + stop]

        parts = [rows(c * count, (c + 1) * count) for c in range(whole)]
        rest = rows(whole * count, whole * count + count // 2)
        rest = jnp.concatenate([rest[:, : LANES // 2], rest[:, LANES // 2 :]], 0)
        return jnp.concatenate([*parts, rest], 1)

    both = [(side, 1 - side) for side in (0, 1)]
    ones = [pair(one_refs[i], got_refs[j], size + one_refs[i].shape[0]) for i, j in both]
    twos = [pair(two_refs[i], got_refs[j], size) for i, j in both]
    for p in (0, 1):
        parts = []
        for at in range(0, size, count):
            parts.append(own_refs[p][at : at + count] + got_refs[p][at : at + count])
        own = jnp.concatenate(parts, 1)
        for q in (0, 1):
            g = 2 * p + q
            blocks = [None] * DP
            for n, c in enumerate(OWN):
                at = (q * len(OWN) + n) * count
                blocks[c] = own[:, at : at + count]
            group = slice(g * count, (g + 1) * count)
            blocks[1], blocks[2] = ones[0][:, group], twos[0][:, group]
            blocks[7], blocks[6] = ones[1][:, group].T, twos[1][:, group].T
            row = jnp.concatenate(blocks, 1)
            row = pltpu.roll(row, me_ref[0] * count, 1)
            out_ref[:, g * width : (g + 1) * width] = row * factor


def finish(me, own, ones, twos, got, count, factor):
    vmem = pl.BlockSpec(memory_space=pltpu.VMEM)
    return pl.pallas_call(
        functools.partial(finish_kernel, factor),
        in_specs=[pl.BlockSpec(memory_space=pltpu.SMEM)] + [vmem] * 8,
        out_specs=vmem,
        out_shape=jax.ShapeDtypeStruct((count, GROUPS * DP * count), jnp.float32),
        compiler_params=pltpu.CompilerParams(vmem_limit_bytes=PRODUCT_VMEM_LIMIT),
    )(me, *own, *ones, *twos, *got)


def on_device(grads, groups, acts):
    me = lax.axis_index("dp").astype(jnp.int32)
    cols = acts[0]
    tokens, width = cols.shape
    rows = width // DP
    turned = cols.T
    peak = jnp.max(jnp.abs(turned), axis=0, keepdims=True).astype(jnp.float32)
    turned = lax.dynamic_slice_in_dim(jnp.concatenate([turned, turned], 0), me * rows, width, 0)
    weight, turned, peak = section_weights(grads[0], groups, (turned, peak))

    size = width // LANES * rows
    pair = GROUPS * rows * rows // LANES
    long, short = size + pair + 8, pair + 8

    top, ahead0 = first_sums(weight, turned, peak, 3, 5, short)
    top = top[:1]
    way, both = (1, -1), (0, 1)
    scaled, begin = products(weight, turned, long, [(3, 1, 3, 4), (5, 0, 4, 5)])
    sums = {(2, 0): begin[0], (2, 1): begin[1]}
    bits = 15 - (tokens * DP - 1).bit_length()

    def pack(value, level):
        room = lax.broadcasted_iota(jnp.int32, value.shape, 0) >= value.shape[0] - 8
        return jnp.where(room, level, value * jnp.exp2(bits - level)).astype(SENT)

    def tag_of(value):
        return value[-1:].astype(jnp.float32)

    def unpack(value):
        return value.astype(jnp.float32) * jnp.exp2(tag_of(value) - bits)

    def send(packed):
        return [shift(packed[i], "dp", way[i]) for i in both]

    start = shift(pack(ahead0, top), "dp", 1)
    got, sent = {}, {}
    sent[2] = [pack(sums[2, i], top) for i in both]
    got[2] = send(sent[2])

    def later(*steps):
        nonlocal scaled
        scaled = lax.optimization_barrier((scaled, *(v for pair in sent.values() for v in pair)))[0]
        jobs = []
        for k in steps:
            ahead, behind, distance = (2 - k // 2, k // 2 - 4, 2) if k % 2 else (4 - k // 2, k // 2 - 5, 1)
            block = (8 - k) // 2 + k % 2
            for i, one in enumerate((ahead, behind)):
                half = i if k == 8 else (k + 1 + i) % 2
                jobs.append((block * way[i], half, one, one + distance))
        result = products(scaled, turned, long, jobs)[0]
        for n, k in enumerate(steps):
            for i in both:
                sums[k, i] = result[2 * n + i]
        return [result]

    def tie(k, *others):
        got[k] = lax.optimization_barrier((*got[k], *others))[:2]

    later(1)
    begun = jnp.pad(unpack(start)[:pair], ((size, 8), (0, 0)))
    sent[1] = [pack(sums[1, 0] + begun, jnp.maximum(top, tag_of(start))), pack(sums[1, 1], top)]
    got[1] = send(sent[1])
    tie(2, *later(3, 4))
    kept = {}
    for k in (4, 3, 6, 5, 7):
        before = [unpack(got[k - 2][i]) for i in both]
        value = [sums[k, i] + before[i] for i in both]
        level = [jnp.maximum(top, tag_of(got[k - 2][i])) for i in both]
        if k == 5:
            kept[2] = [v[size : size + pair] for v in value]
        if k == 7:
            even = [unpack(got[6][i]) for i in both]
            kept[1] = [(sums[8, i] + even[i])[size : size + pair] for i in both]
            own = [sums[8, i][:size] + even[1 - i][:size] for i in both]
            level = [jnp.maximum(level[i], tag_of(got[6][i])) for i in both]
            room = jnp.zeros((16, LANES), jnp.float32)
            value = [jnp.concatenate([value[i][:-8], kept[1][i], room], 0) for i in both]
        sent[k] = [pack(value[i], level[i]) for i in both]
        got[k] = send(sent[k])
        if k == 4:
            tie(1, *sent[k])
        elif k == 3:
            tie(4, *later(5, 6))
        elif k == 6:
            tie(3, *later(7, 8))
        elif k < 7:
            tie(9 - k if k == 6 else k + 1, *sent[k])

    factor = 1.0 / (tokens * DP)
    end = [unpack(got[7][i]) for i in both]
    return finish(me.reshape(1), own, kept[1], kept[2], end, rows, factor)[None]


def solution(mesh):
    return jax.shard_map(
        on_device,
        mesh=mesh,
        in_specs=(
            P("section", "dp", "tensor"),
            P("section", "tensor"),
            P("section", "dp", "tensor"),
        ),
        out_specs=P("section", ("tensor", "dp"), None),
        check_vma=False,
    )
```
